32 devices in a mesh: parts: 2 (over x), wave: 8 (over z, y), pos: 2 (over core).
Axes of the slice: x: 2, y: 2, z: 4, core: 2. Of those that a mesh axis runs over, the one named last changes fastest.
Arguments:
- object_field: float32 [2, 1536, 768], P(None, 'parts'), parts along dimension 1, may hold values from -4 to 4
- probe_field: float32 [8, 2, 1024, 512], P('wave', None, 'parts'), parts along dimension 2, may hold values from -4.5 to 4.5
- resample_blocks: bfloat16 [8, 8, 64, 128], P('wave'), may hold values from -0.5 to 0.5
- band_start: int32 [8, 8], P('wave'), may hold values from 0 to 6
- measured_amplitude: bfloat16 [2, 1024, 512], P('pos', 'parts'), parts along dimension 1, may hold values from 0 to 3.1875
- patch_offsets: int32 [4, 2], P('parts', 'pos'), parts along dimension 0, may hold values from 0 to 256
Outputs:
- object_grad: float32 [2, 1536, 768], P(None, ('parts', 'wave', 'pos')), parts along dimension 1
- probe_grad: float32 [8, 2, 1024, 512], P('wave', None, 'parts'), parts along dimension 2
The draws below stay inside these ranges and needn't reach their ends.
There are 2 independent parts, one for each index of `parts`. The reference program is written for one: setup_inputs(seed, part) draws one part's arguments, and reference() takes and returns one part's arrays. A program takes and returns all parts, laid end to end along the dimension named above; an argument that names none is the same for every part. Nothing has to cross between parts.
All inputs are finite; a program needn't handle non-finite values.
Results may differ from the reference program's by a relative error of at most 0.013.
Values sent between devices are 32-bit elements; how exact they have to be, the bound alone decides.
A program may use at most 128 MiB of HBM per device.

```python
import math
import jax
import jax.numpy as jnp
from jax import lax

M = 512
K = 512
B = 64
BAND = 2
BW = 128
MB = 8
KB = 8
WAVES = 8
POSITIONS = 2
OBJ = 768


def draw_probe_field(key, part):
    key = jax.random.fold_in(key, 11)
    levels = jnp.arange(WAVES, dtype=jnp.float32) / max(WAVES - 1, 1)
    amplitude = 0.6 + 1.2 * levels
    values = 0.7 * jnp.clip(jax.random.normal(key, (WAVES, 2, M, M), jnp.float32), -3.5, 3.5)
    return amplitude[:, None, None, None] * values


def place_ends(entries, own_key, low, top_value):
    longest = entries.shape.index(max(entries.shape))
    spots = []
    for shift in (0, 1):
        where = [jax.random.randint(jax.random.fold_in(own_key, axis), (), 0, length) for axis, length in enumerate(entries.shape)]
        where[longest] = (where[longest] + shift) % entries.shape[longest]
        spots.append(tuple(where))
    return entries.at[spots[0]].set(low).at[spots[1]].set(top_value)


def steps_of(key, extent, pieces, least, high):
    factor_of = 1.0
    for dim, blocks in pieces:
        heights = jax.random.uniform(jax.random.fold_in(jax.random.fold_in(key, 6), dim), (blocks,), jnp.float32, least / len(pieces), high / len(pieces))
        factor_of = factor_of * jnp.repeat(jnp.exp(heights), extent[dim] // blocks).reshape((-1,) + (1,) * (len(extent) - 1 - dim))
    return factor_of


def scatter_about(own_key, shape, scale, limit, cuts=(), kind=jnp.bfloat16):
    gain = steps_of(own_key, shape, cuts, -0.22, 0.18) if cuts else 1.0
    values = jax.random.normal(own_key, shape, jnp.float32) * scale * gain
    return jnp.minimum(jnp.maximum(values, -limit), limit).astype(kind)


def setup_inputs(seed: int = 0, part: int = 0) -> dict:
    arg_keys = jax.random.split(jax.random.key(seed), 7)
    part_keys = jax.random.split(jax.random.fold_in(arg_keys[6], part), 7)
    return {
        "object_field": scatter_about(part_keys[0], (2, OBJ, OBJ), 0.7, 4.0, (), jnp.float32),
        "probe_field": draw_probe_field(jax.random.fold_in(jax.random.fold_in(arg_keys[6], part), 71), part),
        "resample_blocks": scatter_about(arg_keys[2], (WAVES, KB, B, BW), BW ** -0.5, 0.5, ((0, 8),)),
        "band_start": place_ends(jax.random.randint(arg_keys[3], (WAVES, KB), 0, MB - BAND + 1), jax.random.fold_in(arg_keys[3], 1), 0, MB - BAND).astype(jnp.int32),
        "measured_amplitude": jnp.clip(3.1875 * jax.random.uniform(part_keys[4], (POSITIONS, K, K), jnp.float32) ** steps_of(part_keys[4], (POSITIONS, K, K), ((0, 2),), -0.2, 0.2), 0.0, 3.1875).astype(jnp.bfloat16),
        "patch_offsets": place_ends(jax.random.randint(part_keys[5], (2, POSITIONS), 0, OBJ - M + 1), jax.random.fold_in(part_keys[5], 1), 0, OBJ - M).astype(jnp.int32),
    }


def round_low(values):
    return lax.optimization_barrier(values.astype(jnp.bfloat16)).astype(jnp.float32)

def dft_table(length, flip_sign):
    index_line = jnp.arange(length, dtype=jnp.int32)
    phase_steps = index_line[:, None] * index_line[None, :] % length
    angles = phase_steps.astype(jnp.float32) * (2.0 * math.pi / length)
    scaling = 1.0 / math.sqrt(length)
    real_part = jnp.cos(angles) * scaling
    imag_part = flip_sign * jnp.sin(angles) * scaling
    matrix = jnp.stack([jnp.stack([real_part, -imag_part]), jnp.stack([imag_part, real_part])])
    return matrix.astype(jnp.bfloat16)

def band_picker(starts, band_count, block_count):
    band_steps = jnp.arange(band_count, dtype=jnp.int32)
    targets = starts.astype(jnp.int32)[:, None] + band_steps[None, :]
    columns = jnp.arange(block_count, dtype=jnp.int32)
    return (targets[:, :, None] == columns[None, None, :]).astype(jnp.float32)

def dense_resample(blocks, starts):
    picker = band_picker(starts, BAND, MB)
    grouped = blocks.astype(jnp.float32).reshape(KB, B, BAND, B)
    dense_map = jnp.einsum('kbtc,ktn->kbnc', grouped, picker, precision=lax.Precision.HIGHEST)
    return dense_map.reshape(K, M)

def exit_wave(probe_wave, patches):
    real_part = probe_wave[0] * patches[:, 0] - probe_wave[1] * patches[:, 1]
    imag_part = probe_wave[0] * patches[:, 1] + probe_wave[1] * patches[:, 0]
    return jnp.stack([real_part, imag_part], axis=1)

def patch_corner(patch_offsets, position):
    zero_index = jnp.zeros((), jnp.int32)
    return (zero_index, patch_offsets[0, position].astype(jnp.int32), patch_offsets[1, position].astype(jnp.int32))

def reference(object_field, probe_field, resample_blocks, band_start, measured_amplitude, patch_offsets):
    forward_matrix = dft_table(M, -1.0).astype(jnp.float32)
    inverse_matrix = dft_table(M, 1.0).astype(jnp.float32)
    corners = [patch_corner(patch_offsets, position) for position in range(POSITIONS)]
    patches = jnp.stack([lax.dynamic_slice(object_field, corners[position], (2, M, M)) for position in range(POSITIONS)])

    def forward_wave(probe_wave, blocks, starts):
        dense_map = dense_resample(blocks, starts)
        exit_field = round_low(exit_wave(probe_wave, patches))
        half_step = round_low(jnp.einsum('dcxm,pcmy->pdxy', forward_matrix, exit_field))
        far_field = round_low(jnp.einsum('pcxm,dcmy->pdxy', half_step, forward_matrix))
        resampled = round_low(jnp.einsum('km,pcmy->pcky', dense_map, far_field))
        return (jnp.einsum('pcxm,km->pcxk', resampled, dense_map), dense_map)

    def intensity_step(carry, inputs):
        detector_field = forward_wave(inputs[0], inputs[1], inputs[2])[0]
        return (carry + lax.optimization_barrier(jnp.sum(detector_field * detector_field, axis=1)), None)
    intensity_sum = lax.scan(intensity_step, jnp.zeros((POSITIONS, K, K), probe_field.dtype), (probe_field, resample_blocks, band_start))[0]
    factor = 1.0 - measured_amplitude.astype(jnp.float32) / jnp.sqrt(intensity_sum / WAVES + 1.0)

    def backward_step(carry, inputs):
        probe_wave = inputs[0]
        detector_field, dense_map = forward_wave(inputs[0], inputs[1], inputs[2])
        detector_grad = round_low(factor[:, None] * detector_field)
        row_grad = round_low(jnp.einsum('pcxk,km->pcxm', detector_grad, dense_map))
        far_grad = round_low(jnp.einsum('km,pckx->pcmx', dense_map, row_grad))
        half_grad = round_low(jnp.einsum('pcxm,dcmy->pdxy', far_grad, inverse_matrix))
        exit_grad = jnp.einsum('dcxm,pcmy->pdxy', inverse_matrix, half_grad)
        patch_real = probe_wave[0] * exit_grad[:, 0] + probe_wave[1] * exit_grad[:, 1]
        patch_imag = probe_wave[0] * exit_grad[:, 1] - probe_wave[1] * exit_grad[:, 0]
        probe_real = lax.optimization_barrier(jnp.sum(patches[:, 0] * exit_grad[:, 0] + patches[:, 1] * exit_grad[:, 1], axis=0))
        probe_imag = lax.optimization_barrier(jnp.sum(patches[:, 0] * exit_grad[:, 1] - patches[:, 1] * exit_grad[:, 0], axis=0))
        return (carry + jnp.stack([patch_real, patch_imag], axis=1), jnp.stack([probe_real, probe_imag]))
    patch_total, probe_grad = lax.scan(backward_step, jnp.zeros((POSITIONS, 2, M, M), probe_field.dtype), (probe_field, resample_blocks, band_start))
    patch_total = patch_total / WAVES
    object_grad = jnp.zeros((2, OBJ, OBJ), object_field.dtype)
    for position in range(POSITIONS):
        current = lax.dynamic_slice(object_grad, corners[position], (2, M, M))
        object_grad = lax.dynamic_update_slice(object_grad, current + patch_total[position].astype(object_grad.dtype), corners[position])
    return (object_grad, probe_grad)
```

```python
import functools
import math

import jax
import jax.numpy as jnp
import numpy as np
from jax import lax
from jax.experimental import pallas as pl
from jax.experimental.pallas import tpu as pltpu
from jax.sharding import PartitionSpec as P

MESH = pl.DeviceIdType.MESH
LANES = 4
VMEM_BYTES = 52 * 1024 * 1024
F32 = jnp.float32
BF16 = jnp.bfloat16


def dft_tables(length):
    line = np.arange(length, dtype=np.int64)
    angles = (line[:, None] * line[None, :] % length) * (2.0 * math.pi / length)
    real = np.cos(angles) / math.sqrt(length)
    imag = -np.sin(angles) / math.sqrt(length)
    right = np.block([[real, imag], [-imag, real]]).astype(np.float32).astype(jnp.bfloat16)
    left = np.block([[real, -imag], [imag, real]]).astype(np.float32).astype(jnp.bfloat16)
    return jnp.asarray(left), jnp.asarray(right)


def bit_count(waves):
    return waves.bit_length() - 1


def bit_order(lane, bits):
    order = list(range(bits))
    if lane % 2 and bits > 1:
        order[0], order[1] = 1, 0
    return order


def slot_of(chunk, lane, bits):
    slot = 0
    for bit in bit_order(lane, bits):
        slot = slot * 2 + (chunk >> bit) % 2
    return slot


def dot(a, b, contract=((1,), (0,))):
    return lax.dot_general(a, b, (contract, ((), ())), preferred_element_type=F32)


def forward_kernel(
    waves, off_ref, band_ref, obj_ref, probe_ref, blk_ref, left_ref, right_ref,
    patch_ref, det_ref, map_ref, inten_ref, exit_s, half_s, far_s, rows_s,
):
    side = probe_ref.shape[1]
    obj_side = obj_ref.shape[2]
    bits = bit_count(waves)
    tile = 64
    row0 = off_ref[0, 0]
    base = jnp.minimum(row0 // 8 * 8, obj_side - side - 8)
    lift = tile + 8 - (row0 - base)
    shift = lax.rem(obj_side - off_ref[1, 0], obj_side)
    for t in range(side // tile):
        rows = pl.ds(t * tile, tile)
        parts = []
        for c in range(2):
            wide = obj_ref[c, pl.ds(pl.multiple_of(base + t * tile, 8), tile + 8), :]
            part = pltpu.roll(wide, shift, axis=1)[:, :side]
            part = pltpu.roll(part, lax.rem(lift, tile + 8), axis=0)[:tile]
            patch_ref[c, rows, :] = part
            parts.append(part)
        pr, pi = probe_ref[0, rows, :], probe_ref[1, rows, :]
        exit_s[rows, :] = (pr * parts[0] - pi * parts[1]).astype(BF16)
        exit_s[pl.ds(side + t * tile, tile), :] = (pr * parts[1] + pi * parts[0]).astype(BF16)
    blocks, brows, bwidth = blk_ref.shape
    lane_block = lax.broadcasted_iota(jnp.int32, (brows, side), 1) // brows
    for k in range(blocks):
        start = band_ref[0, k]
        blk = blk_ref[k].astype(F32)
        swapped = jnp.concatenate([blk[:, brows:], blk[:, :brows]], axis=1)
        odd = (start % 2).astype(F32)
        chosen = jnp.where(odd > 0.5, swapped, blk)
        wide = jnp.concatenate([chosen] * (side // bwidth), axis=1)
        inside = (lane_block >= start) & (lane_block < start + bwidth // brows)
        map_ref[pl.ds(k * brows, brows), :] = jnp.where(inside, wide, 0.0).astype(BF16)
    step = 256
    per = side // step
    for t in range(2 * per):
        out = dot(left_ref[pl.ds(t * step, step), :], exit_s[...])
        half_s[pl.ds((t % per) * step, step), pl.ds((t // per) * side, side)] = out.astype(BF16)
    for t in range(per):
        rows = pl.ds(t * step, step)
        far_s[rows, :] = dot(half_s[rows, :], right_ref[...]).astype(BF16)
    for t in range(per):
        out = dot(map_ref[pl.ds(t * step, step), :], far_s[...]).astype(BF16)
        rows_s[pl.ds(t * step, step), :] = out[:, :side]
        rows_s[pl.ds(side + t * step, step), :] = out[:, side:]
    height = side // waves
    width = side // LANES
    for t in range(per):
        total = None
        for c in range(2):
            rows = pl.ds(c * side + t * step, step)
            out = dot(rows_s[rows, :], map_ref[...], ((1,), (1,)))
            det_ref[rows, :] = out
            total = out * out if total is None else total + out * out
        for j in range(step // height):
            chunk = t * (step // height) + j
            for lane in range(LANES):
                inten_ref[lane, slot_of(chunk, lane, bits)] = total[
                    j * height : (j + 1) * height, lane * width : (lane + 1) * width
                ]


class Halving:
    def __init__(self, waves, buf, land, send, recv):
        self.bits = bit_count(waves)
        self.waves, self.buf, self.land, self.send, self.recv = waves, buf, land, send, recv
        self.me = lax.axis_index("wave")

    def bit(self, lane, step):
        return (self.me // 2 ** bit_order(lane, self.bits)[step]) % 2

    def partner(self, lane, step):
        return self.me + (1 - 2 * self.bit(lane, step)) * 2 ** bit_order(lane, self.bits)[step]

    def base(self, lane, step):
        return sum((self.bit(lane, s) * (self.waves >> (s + 1)) for s in range(step)), 0)

    def down(self, lane, step):
        half = self.waves >> (step + 1)
        first = self.base(lane, step) + (1 - self.bit(lane, step)) * half
        return pltpu.make_async_remote_copy(
            src_ref=self.buf.at[lane, pl.ds(first, half)],
            dst_ref=self.land.at[lane, pl.ds(half, half)],
            send_sem=self.send.at[lane, step],
            recv_sem=self.recv.at[lane, step],
            device_id={"wave": self.partner(lane, step)},
            device_id_type=MESH,
        )

    def add(self, lane, step):
        half = self.waves >> (step + 1)
        first = self.base(lane, step + 1)
        for k in range(half):
            self.buf[lane, first + k] = self.buf[lane, first + k] + self.land[lane, half + k]

    def up(self, full, lane, step):
        half = self.waves >> (step + 1)
        mine = pl.ds(self.base(lane, step + 1), half)
        return pltpu.make_async_remote_copy(
            src_ref=full.at[lane, mine],
            dst_ref=full.at[lane, mine],
            send_sem=self.send.at[lane, self.bits + step],
            recv_sem=self.recv.at[lane, self.bits + step],
            device_id={"wave": self.partner(lane, step)},
            device_id_type=MESH,
        )


def greet(waves, cores):
    bits = bit_count(waves)
    me = lax.axis_index("wave")
    barrier = pltpu.get_barrier_semaphore()
    for b in range(bits):
        other = me + (1 - 2 * ((me // 2**b) % 2)) * 2**b
        pl.semaphore_signal(barrier, inc=1, device_id={"wave": other}, device_id_type=MESH)
    if cores:
        pl.semaphore_signal(
            barrier, inc=1, device_id={"pos": 1 - lax.axis_index("pos")}, device_id_type=MESH
        )
    pl.semaphore_wait(barrier, bits + int(cores))


def sum_kernel(waves, in_ref, out_ref, buf, land, full, send, recv):
    bits = bit_count(waves)
    ring = Halving(waves, buf, land, send, recv)
    greet(waves, False)
    buf[...] = in_ref[...]
    copies = []
    flying = {}
    for step in range(bits):
        for lane in range(LANES):
            if step:
                flying[lane].wait_recv()
                ring.add(lane, step - 1)
            copy = ring.down(lane, step)
            copy.start()
            flying[lane] = copy
            copies.append(copy)
    for step in reversed(range(bits)):
        for lane in range(LANES):
            flying[lane].wait_recv()
            if step == bits - 1:
                spot = ring.base(lane, bits)
                full[lane, spot] = buf[lane, spot] + land[lane, 1]
            copy = ring.up(full, lane, step)
            copy.start()
            flying[lane] = copy
            copies.append(copy)
    for lane in range(LANES):
        flying[lane].wait_recv()
    for copy in copies:
        copy.wait_send()
    out_ref[...] = full[...]


def backward_kernel(
    waves, off_ref, det_ref, total_ref, meas_ref, map_ref, patch_ref, probe_ref, left_ref, right_ref,
    term_ref, place_ref, grad_s, row_s, far_s, half_s, pad_s,
):
    side = probe_ref.shape[1]
    obj_side = pad_s.shape[2]
    margin = obj_side - side
    bits = bit_count(waves)
    height = side // waves
    width = side // LANES
    for chunk in range(waves):
        rows = pl.ds(chunk * height, height)
        total = jnp.concatenate(
            [total_ref[lane, slot_of(chunk, lane, bits)] for lane in range(LANES)], axis=1
        )
        factor = 1.0 - meas_ref[rows, :].astype(F32) / jnp.sqrt(total * (1.0 / waves) + 1.0)
        for c in range(2):
            there = pl.ds(c * side + chunk * height, height)
            grad_s[there, :] = (factor * det_ref[there, :]).astype(BF16)
    for c in range(2):
        pad_s[c, pl.ds(0, margin), :] = jnp.zeros((margin, obj_side), F32)
        pad_s[c, pl.ds(margin + side, margin + 16), :] = jnp.zeros((margin + 16, obj_side), F32)
    step = 256
    per = side // step
    for t in range(2 * per):
        out = dot(grad_s[pl.ds(t * step, step), :], map_ref[...])
        row_s[pl.ds((t % per) * step, step), pl.ds((t // per) * side, side)] = out.astype(BF16)
    for t in range(per):
        rows = pl.ds(t * step, step)
        far_s[rows, :] = dot(map_ref[:, t * step : (t + 1) * step], row_s[...], ((0,), (0,))).astype(BF16)
    for t in range(per):
        rows = pl.ds(t * step, step)
        out = dot(far_s[rows, :], left_ref[...]).astype(BF16)
        half_s[rows, :] = out[:, :side]
        half_s[pl.ds(side + t * step, step), :] = out[:, side:]
    shift = off_ref[1, 0]
    scale = 1.0 / waves
    fill = jnp.zeros((step, margin), F32)
    for t in range(per):
        rows = pl.ds(t * step, step)
        er = dot(right_ref[rows, :], half_s[...])
        ei = dot(right_ref[pl.ds(side + t * step, step), :], half_s[...])
        ar, ai = patch_ref[0, rows, :], patch_ref[1, rows, :]
        term_ref[0, rows, :] = ar * er + ai * ei
        term_ref[1, rows, :] = ar * ei - ai * er
        pr, pi = probe_ref[0, rows, :], probe_ref[1, rows, :]
        real = (pr * er + pi * ei) * scale
        imag = (pr * ei - pi * er) * scale
        pad_s[0, pl.ds(margin + t * step, step), :] = pltpu.roll(
            jnp.concatenate([real, fill], axis=1), shift, axis=1
        )
        pad_s[1, pl.ds(margin + t * step, step), :] = pltpu.roll(
            jnp.concatenate([imag, fill], axis=1), shift, axis=1
        )
    tall = place_ref.shape[3]
    wide = place_ref.shape[4]
    first = margin - off_ref[0, 0]
    for c in range(2):
        for owner in range(2 * waves):
            start = first + owner * tall
            tiles = (tall + 7) // 8 * 8 + 8
            block = pad_s[c, pl.ds(pl.multiple_of(start // 8 * 8, 8), tiles), :]
            block = pltpu.roll(block, lax.rem(tiles - start % 8, tiles), axis=0)[:tall]
            for part in range(LANES // 2):
                lane = 2 * part + c
                place_ref[owner % 2, lane, slot_of(owner // 2, lane, bits)] = block[
                    :, part * wide : (part + 1) * wide
                ]


def scatter_kernel(
    waves, place_ref, term_ref, obj_ref, probe_ref, buf, land, cross, other, send, recv, csend, crecv
):
    bits = bit_count(waves)
    ring = Halving(waves, buf, land, send, recv)
    mine = lax.axis_index("pos")
    greet(waves, True)

    def to_core(source, target, index):
        return pltpu.make_async_remote_copy(
            src_ref=source, dst_ref=target, send_sem=csend.at[index], recv_sem=crecv.at[index],
            device_id={"pos": 1 - mine}, device_id_type=MESH,
        )

    swaps = [to_core(place_ref.at[1 - mine, lane], cross.at[lane], lane) for lane in range(LANES)]
    terms = [to_core(term_ref.at[c], other.at[c], LANES + c) for c in range(2)]
    for copy in swaps + terms:
        copy.start()
    copies = swaps + terms
    flying = {}
    for step in range(bits):
        for lane in range(LANES):
            if step:
                flying[lane].wait_recv()
                ring.add(lane, step - 1)
            else:
                swaps[lane].wait_recv()
                for k in range(waves):
                    buf[lane, k] = place_ref[mine, lane, k] + cross[lane, k]
            copy = ring.down(lane, step)
            copy.start()
            flying[lane] = copy
            copies.append(copy)
    for c in range(2):
        terms[c].wait_recv()
        probe_ref[c] = term_ref[c] + other[c]
    wide = buf.shape[3]
    for lane in range(LANES):
        flying[lane].wait_recv()
        spot = ring.base(lane, bits)
        obj_ref[lane % 2, :, pl.ds((lane // 2) * wide, wide)] = buf[lane, spot] + land[lane, 1]
    for copy in copies:
        copy.wait_send()


def local(waves, object_field, probe_field, resample_blocks, band_start, measured, offsets):
    side = probe_field.shape[2]
    obj_side = object_field.shape[1]
    bits = bit_count(waves)
    left, right = dft_tables(side)
    probe = probe_field[0]
    vmem = pl.BlockSpec(memory_space=pltpu.VMEM)
    smem = pl.BlockSpec(memory_space=pltpu.SMEM)
    shape = jax.ShapeDtypeStruct
    plain = pltpu.CompilerParams(vmem_limit_bytes=VMEM_BYTES)
    lanes_shape = (LANES, waves, side // waves, side // LANES)
    patch, det, dense, inten = pl.pallas_call(
        functools.partial(forward_kernel, waves),
        out_shape=(
            shape((2, side, side), F32), shape((2 * side, side), F32), shape((side, side), BF16),
            shape(lanes_shape, F32),
        ),
        in_specs=[smem, smem] + [vmem] * 5,
        out_specs=(vmem,) * 4,
        scratch_shapes=[
            pltpu.VMEM((2 * side, side), BF16), pltpu.VMEM((side, 2 * side), BF16),
            pltpu.VMEM((side, 2 * side), BF16), pltpu.VMEM((2 * side, side), BF16),
        ],
        compiler_params=plain,
        name="forward",
    )(offsets, band_start, object_field, probe, resample_blocks[0], left, right)
    total = pl.pallas_call(
        functools.partial(sum_kernel, waves),
        out_shape=shape(lanes_shape, F32),
        in_specs=[vmem],
        out_specs=vmem,
        scratch_shapes=[
            pltpu.VMEM(lanes_shape, F32), pltpu.VMEM(lanes_shape, F32), pltpu.VMEM(lanes_shape, F32),
            pltpu.SemaphoreType.DMA((LANES, 2 * bits)), pltpu.SemaphoreType.DMA((LANES, 2 * bits)),
        ],
        compiler_params=pltpu.CompilerParams(
            vmem_limit_bytes=VMEM_BYTES, collective_id=0, has_side_effects=True
        ),
        name="intensity_sum",
    )(inten)
    tall = obj_side // (2 * waves)
    wide = 2 * obj_side // LANES
    place_shape = (LANES, waves, tall, wide)
    term, place = pl.pallas_call(
        functools.partial(backward_kernel, waves),
        out_shape=(shape((2, side, side), F32), shape((2,) + place_shape, F32)),
        in_specs=[smem] + [vmem] * 8,
        out_specs=(vmem,) * 2,
        scratch_shapes=[
            pltpu.VMEM((2 * side, side), BF16), pltpu.VMEM((side, 2 * side), BF16),
            pltpu.VMEM((side, 2 * side), BF16), pltpu.VMEM((2 * side, side), BF16),
            pltpu.VMEM((2, 2 * obj_side - side + 16, obj_side), F32),
        ],
        compiler_params=plain,
        name="backward",
    )(offsets, det, total, measured[0], dense, patch, probe, left, right)
    object_grad, probe_grad = pl.pallas_call(
        functools.partial(scatter_kernel, waves),
        out_shape=(shape((2, tall, obj_side), F32), shape((2, side, side), F32)),
        in_specs=[vmem] * 2,
        out_specs=(vmem,) * 2,
        scratch_shapes=[
            pltpu.VMEM(place_shape, F32), pltpu.VMEM(place_shape, F32), pltpu.VMEM(place_shape, F32),
            pltpu.VMEM((2, side, side), F32),
            pltpu.SemaphoreType.DMA((LANES, bits)), pltpu.SemaphoreType.DMA((LANES, bits)),
            pltpu.SemaphoreType.DMA((LANES + 2,)), pltpu.SemaphoreType.DMA((LANES + 2,)),
        ],
        compiler_params=pltpu.CompilerParams(
            vmem_limit_bytes=VMEM_BYTES, collective_id=1, has_side_effects=True
        ),
        name="object_sum",
    )(place, term)
    return object_grad, probe_grad[None]


def solution(mesh):
    in_specs = (
        P(None, "parts", None),
        P("wave", None, "parts", None),
        P("wave", None, None, None),
        P("wave", None),
        P("pos", "parts", None),
        P("parts", "pos"),
    )
    out_specs = (P(None, ("parts", "wave", "pos"), None), P("wave", None, "parts", None))
    step = functools.partial(local, mesh.shape["wave"])
    return jax.shard_map(step, mesh=mesh, in_specs=in_specs, out_specs=out_specs, check_vma=False)
```

```python
import functools
import math

import jax
import jax.numpy as jnp
import numpy as np
from jax import lax
from jax.experimental import pallas as pl
from jax.experimental.pallas import tpu as pltpu
from jax.sharding import PartitionSpec as P

MESH = pl.DeviceIdType.MESH
SUM_LANES = 8
GROUP = 100
MIX = 2
VMEM_BYTES = 52 * 1024 * 1024
F32 = jnp.float32
BF16 = jnp.bfloat16


def dft_tables(length):
    line = np.arange(length, dtype=np.int64)
    angles = (line[:, None] * line[None, :] % length) * (2.0 * math.pi / length)
    real = np.cos(angles) / math.sqrt(length)
    imag = -np.sin(angles) / math.sqrt(length)
    right = np.block([[real, imag], [-imag, real]]).astype(np.float32).astype(jnp.bfloat16)
    left = np.block([[real, -imag], [imag, real]]).astype(np.float32).astype(jnp.bfloat16)
    return jnp.asarray(left), jnp.asarray(right)


def bit_count(waves):
    return waves.bit_length() - 1


def bit_order(lane, bits):
    order = list(range(bits))
    if lane % MIX == MIX - 1 and bits > 1:
        order[0], order[1] = 1, 0
    return order


def slot_of(chunk, lane, bits):
    slot = 0
    for bit in bit_order(lane, bits):
        slot = slot * 2 + (chunk >> bit) % 2
    return slot


def dot(a, b, contract=((1,), (0,))):
    return lax.dot_general(a, b, (contract, ((), ())), preferred_element_type=F32)


def forward_kernel(
    waves, off_ref, band_ref, obj_ref, probe_ref, blk_ref, left_ref, right_ref,
    patch_ref, det_ref, map_ref, inten_ref, exit_s, half_s, far_s, rows_s,
):
    side = probe_ref.shape[1]
    obj_side = obj_ref.shape[2]
    bits = bit_count(waves)
    tile = 64
    row0 = off_ref[0, 0]
    base = jnp.minimum(row0 // 8 * 8, obj_side - side - 8)
    lift = tile + 8 - (row0 - base)
    shift = lax.rem(obj_side - off_ref[1, 0], obj_side)
    for t in range(side // tile):
        rows = pl.ds(t * tile, tile)
        parts = []
        for c in range(2):
            wide = obj_ref[c, pl.ds(pl.multiple_of(base + t * tile, 8), tile + 8), :]
            part = pltpu.roll(wide, shift, axis=1)[:, :side]
            part = pltpu.roll(part, lax.rem(lift, tile + 8), axis=0)[:tile]
            patch_ref[c, rows, :] = part
            parts.append(part)
        pr, pi = probe_ref[0, rows, :], probe_ref[1, rows, :]
        exit_s[rows, :] = (pr * parts[0] - pi * parts[1]).astype(BF16)
        exit_s[pl.ds(side + t * tile, tile), :] = (pr * parts[1] + pi * parts[0]).astype(BF16)
    blocks, brows, bwidth = blk_ref.shape
    lane_block = lax.broadcasted_iota(jnp.int32, (brows, side), 1) // brows
    for k in range(blocks):
        start = band_ref[0, k]
        blk = blk_ref[k].astype(F32)
        swapped = jnp.concatenate([blk[:, brows:], blk[:, :brows]], axis=1)
        odd = (start % 2).astype(F32)
        chosen = jnp.where(odd > 0.5, swapped, blk)
        wide = jnp.concatenate([chosen] * (side // bwidth), axis=1)
        inside = (lane_block >= start) & (lane_block < start + bwidth // brows)
        map_ref[pl.ds(k * brows, brows), :] = jnp.where(inside, wide, 0.0).astype(BF16)
    step = 256
    per = side // step
    for t in range(2 * per):
        out = dot(left_ref[pl.ds(t * step, step), :], exit_s[...])
        half_s[pl.ds((t % per) * step, step), pl.ds((t // per) * side, side)] = out.astype(BF16)
    for t in range(per):
        rows = pl.ds(t * step, step)
        far_s[rows, :] = dot(half_s[rows, :], right_ref[...]).astype(BF16)
    for t in range(per):
        out = dot(map_ref[pl.ds(t * step, step), :], far_s[...]).astype(BF16)
        rows_s[pl.ds(t * step, step), :] = out[:, :side]
        rows_s[pl.ds(side + t * step, step), :] = out[:, side:]
    height = side // waves
    width = side // (SUM_LANES // 2)
    for t in range(per):
        total = None
        for c in range(2):
            rows = pl.ds(c * side + t * step, step)
            out = dot(rows_s[rows, :], map_ref[...], ((1,), (1,)))
            det_ref[rows, :] = out
            total = out * out if total is None else total + out * out
        for j in range(step // height):
            chunk = t * (step // height) + j
            for lane in range(SUM_LANES):
                top = j * height + lane % 2 * (height // 2)
                first = lane // 2 * width
                inten_ref[lane, slot_of(chunk, lane, bits)] = total[
                    top : top + height // 2, first : first + width
                ]


def diagonal(lanes, steps):
    def key(item):
        lane, step = item
        group = lane // GROUP
        return (group - 1 if step == 0 else group + step, step, lane)

    return sorted([(lane, step) for lane in range(lanes) for step in range(steps)], key=key)


class Halving:
    def __init__(self, waves, buf, land, send, recv):
        self.bits = bit_count(waves)
        self.waves, self.buf, self.land, self.send, self.recv = waves, buf, land, send, recv
        self.me = lax.axis_index("wave")

    def bit(self, lane, step):
        return (self.me // 2 ** bit_order(lane, self.bits)[step]) % 2

    def partner(self, lane, step):
        return self.me + (1 - 2 * self.bit(lane, step)) * 2 ** bit_order(lane, self.bits)[step]

    def base(self, lane, step):
        return sum((self.bit(lane, s) * (self.waves >> (s + 1)) for s in range(step)), 0)

    def down(self, lane, step):
        half = self.waves >> (step + 1)
        first = self.base(lane, step) + (1 - self.bit(lane, step)) * half
        return pltpu.make_async_remote_copy(
            src_ref=self.buf.at[lane, pl.ds(first, half)],
            dst_ref=self.land.at[lane, pl.ds(half, half)],
            send_sem=self.send.at[lane, step],
            recv_sem=self.recv.at[lane, step],
            device_id={"wave": self.partner(lane, step)},
            device_id_type=MESH,
        )

    def add(self, lane, step):
        half = self.waves >> (step + 1)
        first = self.base(lane, step + 1)
        for k in range(half):
            self.buf[lane, first + k] = self.buf[lane, first + k] + self.land[lane, half + k]

    def up(self, full, lane, step):
        half = self.waves >> (step + 1)
        mine = pl.ds(self.base(lane, step + 1), half)
        return pltpu.make_async_remote_copy(
            src_ref=full.at[lane, mine],
            dst_ref=full.at[lane, mine],
            send_sem=self.send.at[lane, self.bits + step],
            recv_sem=self.recv.at[lane, self.bits + step],
            device_id={"wave": self.partner(lane, step)},
            device_id_type=MESH,
        )


def greet(waves, cores):
    bits = bit_count(waves)
    me = lax.axis_index("wave")
    barrier = pltpu.get_barrier_semaphore()
    for b in range(bits):
        other = me + (1 - 2 * ((me // 2**b) % 2)) * 2**b
        pl.semaphore_signal(barrier, inc=1, device_id={"wave": other}, device_id_type=MESH)
    if cores:
        pl.semaphore_signal(
            barrier, inc=1, device_id={"pos": 1 - lax.axis_index("pos")}, device_id_type=MESH
        )
    pl.semaphore_wait(barrier, bits + int(cores))


def sum_kernel(waves, in_ref, out_ref, buf, land, full, send, recv):
    bits = bit_count(waves)
    ring = Halving(waves, buf, land, send, recv)
    greet(waves, False)
    buf[...] = in_ref[...]
    copies = []
    flying = {}
    for lane, step in diagonal(SUM_LANES, 2 * bits):
        if step:
            flying[lane].wait_recv()
        if step < bits:
            if step:
                ring.add(lane, step - 1)
            copy = ring.down(lane, step)
        else:
            if step == bits:
                spot = ring.base(lane, bits)
                full[lane, spot] = buf[lane, spot] + land[lane, 1]
            copy = ring.up(full, lane, 2 * bits - 1 - step)
        copy.start()
        flying[lane] = copy
        copies.append(copy)
    for lane in range(SUM_LANES):
        flying[lane].wait_recv()
    for copy in copies:
        copy.wait_send()
    out_ref[...] = full[...]


def backward_kernel(
    waves, off_ref, det_ref, total_ref, meas_ref, map_ref, patch_ref, probe_ref, left_ref, right_ref,
    term_ref, place_ref, grad_s, row_s, far_s, half_s, pad_s,
):
    side = probe_ref.shape[1]
    obj_side = pad_s.shape[2]
    margin = obj_side - side
    bits = bit_count(waves)
    height = side // waves
    for piece in range(2 * waves):
        chunk, half = piece // 2, piece % 2
        rows = pl.ds(piece * (height // 2), height // 2)
        total = jnp.concatenate(
            [total_ref[lane, slot_of(chunk, lane, bits)] for lane in range(half, SUM_LANES, 2)],
            axis=1,
        )
        factor = 1.0 - meas_ref[rows, :].astype(F32) / jnp.sqrt(total * (1.0 / waves) + 1.0)
        for c in range(2):
            there = pl.ds(c * side + piece * (height // 2), height // 2)
            grad_s[there, :] = (factor * det_ref[there, :]).astype(BF16)
    for c in range(2):
        pad_s[c, pl.ds(0, margin), :] = jnp.zeros((margin, obj_side), F32)
        pad_s[c, pl.ds(margin + side, margin + 16), :] = jnp.zeros((margin + 16, obj_side), F32)
    step = 256
    per = side // step
    for t in range(2 * per):
        out = dot(grad_s[pl.ds(t * step, step), :], map_ref[...])
        row_s[pl.ds((t % per) * step, step), pl.ds((t // per) * side, side)] = out.astype(BF16)
    for t in range(per):
        rows = pl.ds(t * step, step)
        far_s[rows, :] = dot(map_ref[:, t * step : (t + 1) * step], row_s[...], ((0,), (0,))).astype(BF16)
    for t in range(per):
        rows = pl.ds(t * step, step)
        out = dot(far_s[rows, :], left_ref[...]).astype(BF16)
        half_s[rows, :] = out[:, :side]
        half_s[pl.ds(side + t * step, step), :] = out[:, side:]
    shift = off_ref[1, 0]
    scale = 1.0 / waves
    fill = jnp.zeros((step, margin), F32)
    for t in range(per):
        rows = pl.ds(t * step, step)
        er = dot(right_ref[rows, :], half_s[...])
        ei = dot(right_ref[pl.ds(side + t * step, step), :], half_s[...])
        ar, ai = patch_ref[0, rows, :], patch_ref[1, rows, :]
        term_ref[0, rows, :] = ar * er + ai * ei
        term_ref[1, rows, :] = ar * ei - ai * er
        pr, pi = probe_ref[0, rows, :], probe_ref[1, rows, :]
        real = (pr * er + pi * ei) * scale
        imag = (pr * ei - pi * er) * scale
        pad_s[0, pl.ds(margin + t * step, step), :] = pltpu.roll(
            jnp.concatenate([real, fill], axis=1), shift, axis=1
        )
        pad_s[1, pl.ds(margin + t * step, step), :] = pltpu.roll(
            jnp.concatenate([imag, fill], axis=1), shift, axis=1
        )
    tall = place_ref.shape[3]
    wide = place_ref.shape[4]
    first = margin - off_ref[0, 0]
    for c in range(2):
        for owner in range(2 * waves):
            start = first + owner * tall
            tiles = (tall + 7) // 8 * 8 + 8
            block = pad_s[c, pl.ds(pl.multiple_of(start // 8 * 8, 8), tiles), :]
            block = pltpu.roll(block, lax.rem(tiles - start % 8, tiles), axis=0)[:tall]
            for part in range(place_ref.shape[1] // 2):
                lane = 2 * part + c
                place_ref[owner % 2, lane, slot_of(owner // 2, lane, bits)] = block[
                    :, part * wide : (part + 1) * wide
                ]


def scatter_kernel(
    waves, place_ref, term_ref, obj_ref, probe_ref, buf, land, cross, other, send, recv, csend, crecv
):
    bits = bit_count(waves)
    ring = Halving(waves, buf, land, send, recv)
    mine = lax.axis_index("pos")
    greet(waves, True)

    def to_core(source, target, index):
        return pltpu.make_async_remote_copy(
            src_ref=source, dst_ref=target, send_sem=csend.at[index], recv_sem=crecv.at[index],
            device_id={"pos": 1 - mine}, device_id_type=MESH,
        )

    lanes = place_ref.shape[1]
    swaps = [to_core(place_ref.at[1 - mine, lane], cross.at[lane], lane) for lane in range(lanes)]
    terms = [to_core(term_ref.at[c], other.at[c], lanes + c) for c in range(2)]
    copies = swaps + terms
    for copy in copies:
        copy.start()
    flying = {}
    for lane, step in diagonal(lanes, bits):
        if step:
            flying[lane].wait_recv()
            ring.add(lane, step - 1)
        else:
            swaps[lane].wait_recv()
            for k in range(waves):
                buf[lane, k] = place_ref[mine, lane, k] + cross[lane, k]
        copy = ring.down(lane, step)
        copy.start()
        flying[lane] = copy
        copies.append(copy)
    for c in range(2):
        terms[c].wait_recv()
        probe_ref[c] = term_ref[c] + other[c]
    wide = buf.shape[3]
    for lane in range(lanes):
        flying[lane].wait_recv()
        spot = ring.base(lane, bits)
        obj_ref[lane % 2, :, pl.ds((lane // 2) * wide, wide)] = buf[lane, spot] + land[lane, 1]
    for copy in copies:
        copy.wait_send()


def local(waves, object_field, probe_field, resample_blocks, band_start, measured, offsets):
    side = probe_field.shape[2]
    obj_side = object_field.shape[1]
    bits = bit_count(waves)
    left, right = dft_tables(side)
    probe = probe_field[0]
    vmem = pl.BlockSpec(memory_space=pltpu.VMEM)
    smem = pl.BlockSpec(memory_space=pltpu.SMEM)
    shape = jax.ShapeDtypeStruct
    plain = pltpu.CompilerParams(vmem_limit_bytes=VMEM_BYTES)
    lanes_shape = (SUM_LANES, waves, side // waves // 2, side // (SUM_LANES // 2))
    patch, det, dense, inten = pl.pallas_call(
        functools.partial(forward_kernel, waves),
        out_shape=(
            shape((2, side, side), F32), shape((2 * side, side), F32), shape((side, side), BF16),
            shape(lanes_shape, F32),
        ),
        in_specs=[smem, smem] + [vmem] * 5,
        out_specs=(vmem,) * 4,
        scratch_shapes=[
            pltpu.VMEM((2 * side, side), BF16), pltpu.VMEM((side, 2 * side), BF16),
            pltpu.VMEM((side, 2 * side), BF16), pltpu.VMEM((2 * side, side), BF16),
        ],
        compiler_params=plain,
        name="forward",
    )(offsets, band_start, object_field, probe, resample_blocks[0], left, right)
    total = pl.pallas_call(
        functools.partial(sum_kernel, waves),
        out_shape=shape(lanes_shape, F32),
        in_specs=[vmem],
        out_specs=vmem,
        scratch_shapes=[
            pltpu.VMEM(lanes_shape, F32), pltpu.VMEM(lanes_shape, F32), pltpu.VMEM(lanes_shape, F32),
            pltpu.SemaphoreType.DMA((SUM_LANES, 2 * bits)),
            pltpu.SemaphoreType.DMA((SUM_LANES, 2 * bits)),
        ],
        compiler_params=pltpu.CompilerParams(
            vmem_limit_bytes=VMEM_BYTES, collective_id=0, has_side_effects=True
        ),
        name="intensity_sum",
    )(inten)
    tall = obj_side // (2 * waves)
    wide = 128
    lanes = 2 * obj_side // wide
    place_shape = (lanes, waves, tall, wide)
    term, place = pl.pallas_call(
        functools.partial(backward_kernel, waves),
        out_shape=(shape((2, side, side), F32), shape((2,) + place_shape, F32)),
        in_specs=[smem] + [vmem] * 8,
        out_specs=(vmem,) * 2,
        scratch_shapes=[
            pltpu.VMEM((2 * side, side), BF16), pltpu.VMEM((side, 2 * side), BF16),
            pltpu.VMEM((side, 2 * side), BF16), pltpu.VMEM((2 * side, side), BF16),
            pltpu.VMEM((2, 2 * obj_side - side + 16, obj_side), F32),
        ],
        compiler_params=plain,
        name="backward",
    )(offsets, det, total, measured[0], dense, patch, probe, left, right)
    object_grad, probe_grad = pl.pallas_call(
        functools.partial(scatter_kernel, waves),
        out_shape=(shape((2, tall, obj_side), F32), shape((2, side, side), F32)),
        in_specs=[vmem] * 2,
        out_specs=(vmem,) * 2,
        scratch_shapes=[
            pltpu.VMEM(place_shape, F32), pltpu.VMEM(place_shape, F32), pltpu.VMEM(place_shape, F32),
            pltpu.VMEM((2, side, side), F32),
            pltpu.SemaphoreType.DMA((lanes, bits)), pltpu.SemaphoreType.DMA((lanes, bits)),
            pltpu.SemaphoreType.DMA((lanes + 2,)), pltpu.SemaphoreType.DMA((lanes + 2,)),
        ],
        compiler_params=pltpu.CompilerParams(
            vmem_limit_bytes=VMEM_BYTES, collective_id=1, has_side_effects=True
        ),
        name="object_sum",
    )(place, term)
    return object_grad, probe_grad[None]


def solution(mesh):
    in_specs = (
        P(None, "parts", None),
        P("wave", None, "parts", None),
        P("wave", None, None, None),
        P("wave", None),
        P("pos", "parts", None),
        P("parts", "pos"),
    )
    out_specs = (P(None, ("parts", "wave", "pos"), None), P("wave", None, "parts", None))
    step = functools.partial(local, mesh.shape["wave"])
    return jax.shard_map(step, mesh=mesh, in_specs=in_specs, out_specs=out_specs, check_vma=False)
```

```python
import functools
import math

import jax
import jax.numpy as jnp
import numpy as np
from jax import lax
from jax.experimental import pallas as pl
from jax.experimental.pallas import tpu as pltpu
from jax.sharding import PartitionSpec as P

MESH = pl.DeviceIdType.MESH
SUM_LANES = 8
GROUP = 100
MIX = 2
VMEM_BYTES = 52 * 1024 * 1024
F32 = jnp.float32
BF16 = jnp.bfloat16


def dft_tables(length):
    line = np.arange(length, dtype=np.int64)
    angles = (line[:, None] * line[None, :] % length) * (2.0 * math.pi / length)
    real = np.cos(angles) / math.sqrt(length)
    imag = -np.sin(angles) / math.sqrt(length)
    right = np.block([[real, imag], [-imag, real]]).astype(np.float32).astype(jnp.bfloat16)
    left = np.block([[real, -imag], [imag, real]]).astype(np.float32).astype(jnp.bfloat16)
    return jnp.asarray(left), jnp.asarray(right)


def bit_count(waves):
    return waves.bit_length() - 1


def bit_order(lane, bits):
    order = list(range(bits))
    if lane % MIX == MIX - 1 and bits > 1:
        order[0], order[1] = 1, 0
    return order


def slot_of(chunk, lane, bits):
    slot = 0
    for bit in bit_order(lane, bits):
        slot = slot * 2 + (chunk >> bit) % 2
    return slot


def dot(a, b, contract=((1,), (0,))):
    return lax.dot_general(a, b, (contract, ((), ())), preferred_element_type=F32)


def forward_kernel(
    waves, off_ref, band_ref, obj_ref, probe_ref, blk_ref, left_ref, right_ref,
    patch_ref, det_ref, map_ref, inten_ref, exit_s, half_s, far_s, rows_s,
):
    side = probe_ref.shape[1]
    obj_side = obj_ref.shape[2]
    bits = bit_count(waves)
    tile = 64
    row0 = off_ref[0, 0]
    base = jnp.minimum(row0 // 8 * 8, obj_side - side - 8)
    lift = tile + 8 - (row0 - base)
    shift = lax.rem(obj_side - off_ref[1, 0], obj_side)
    for t in range(side // tile):
        rows = pl.ds(t * tile, tile)
        parts = []
        for c in range(2):
            wide = obj_ref[c, pl.ds(pl.multiple_of(base + t * tile, 8), tile + 8), :]
            part = pltpu.roll(wide, shift, axis=1)[:, :side]
            part = pltpu.roll(part, lax.rem(lift, tile + 8), axis=0)[:tile]
            patch_ref[c, rows, :] = part
            parts.append(part)
        pr, pi = probe_ref[0, rows, :], probe_ref[1, rows, :]
        exit_s[rows, :] = (pr * parts[0] - pi * parts[1]).astype(BF16)
        exit_s[pl.ds(side + t * tile, tile), :] = (pr * parts[1] + pi * parts[0]).astype(BF16)
    blocks, brows, bwidth = blk_ref.shape
    lane_block = lax.broadcasted_iota(jnp.int32, (brows, side), 1) // brows
    for k in range(blocks):
        start = band_ref[0, k]
        blk = blk_ref[k].astype(F32)
        swapped = jnp.concatenate([blk[:, brows:], blk[:, :brows]], axis=1)
        odd = (start % 2).astype(F32)
        chosen = jnp.where(odd > 0.5, swapped, blk)
        wide = jnp.concatenate([chosen] * (side // bwidth), axis=1)
        inside = (lane_block >= start) & (lane_block < start + bwidth // brows)
        map_ref[pl.ds(k * brows, brows), :] = jnp.where(inside, wide, 0.0).astype(BF16)
    step = 256
    per = side // step
    for t in range(2 * per):
        out = dot(left_ref[pl.ds(t * step, step), :], exit_s[...])
        half_s[pl.ds((t % per) * step, step), pl.ds((t // per) * side, side)] = out.astype(BF16)
    for t in range(per):
        rows = pl.ds(t * step, step)
        far_s[rows, :] = dot(half_s[rows, :], right_ref[...]).astype(BF16)
    for t in range(per):
        out = dot(map_ref[pl.ds(t * step, step), :], far_s[...]).astype(BF16)
        rows_s[pl.ds(t * step, step), :] = out[:, :side]
        rows_s[pl.ds(side + t * step, step), :] = out[:, side:]
    height = side // waves
    width = side // (SUM_LANES // 2)
    for t in range(per):
        total = None
        for c in range(2):
            rows = pl.ds(c * side + t * step, step)
            out = dot(rows_s[rows, :], map_ref[...], ((1,), (1,)))
            det_ref[rows, :] = out
            total = out * out if total is None else total + out * out
        for j in range(step // height):
            chunk = t * (step // height) + j
            for lane in range(SUM_LANES):
                top = j * height + lane % 2 * (height // 2)
                first = lane // 2 * width
                inten_ref[lane, slot_of(chunk, lane, bits)] = total[
                    top : top + height // 2, first : first + width
                ]


def diagonal(lanes, steps):
    def key(item):
        lane, step = item
        group = lane // GROUP
        return (group - 1 if step == 0 else group + step, step, lane)

    return sorted([(lane, step) for lane in range(lanes) for step in range(steps)], key=key)


class Halving:
    def __init__(self, waves, buf, land, send, recv):
        self.bits = bit_count(waves)
        self.waves, self.buf, self.land, self.send, self.recv = waves, buf, land, send, recv
        self.me = lax.axis_index("wave")

    def bit(self, lane, step):
        return (self.me // 2 ** bit_order(lane, self.bits)[step]) % 2

    def partner(self, lane, step):
        return self.me + (1 - 2 * self.bit(lane, step)) * 2 ** bit_order(lane, self.bits)[step]

    def base(self, lane, step):
        return sum((self.bit(lane, s) * (self.waves >> (s + 1)) for s in range(step)), 0)

    def down(self, lane, step):
        half = self.waves >> (step + 1)
        first = self.base(lane, step) + (1 - self.bit(lane, step)) * half
        return pltpu.make_async_remote_copy(
            src_ref=self.buf.at[lane, pl.ds(first, half)],
            dst_ref=self.land.at[lane, pl.ds(half, half)],
            send_sem=self.send.at[lane, step],
            recv_sem=self.recv.at[lane, step],
            device_id={"wave": self.partner(lane, step)},
            device_id_type=MESH,
        )

    def add(self, lane, step):
        half = self.waves >> (step + 1)
        first = self.base(lane, step + 1)
        for k in range(half):
            self.buf[lane, first + k] = self.buf[lane, first + k] + self.land[lane, half + k]

    def up(self, full, lane, step):
        half = self.waves >> (step + 1)
        mine = pl.ds(self.base(lane, step + 1), half)
        return pltpu.make_async_remote_copy(
            src_ref=full.at[lane, mine],
            dst_ref=full.at[lane, mine],
            send_sem=self.send.at[lane, self.bits + step],
            recv_sem=self.recv.at[lane, self.bits + step],
            device_id={"wave": self.partner(lane, step)},
            device_id_type=MESH,
        )


def greet(waves, cores):
    bits = bit_count(waves)
    me = lax.axis_index("wave")
    barrier = pltpu.get_barrier_semaphore()
    for b in range(bits):
        other = me + (1 - 2 * ((me // 2**b) % 2)) * 2**b
        pl.semaphore_signal(barrier, inc=1, device_id={"wave": other}, device_id_type=MESH)
    if cores:
        pl.semaphore_signal(
            barrier, inc=1, device_id={"pos": 1 - lax.axis_index("pos")}, device_id_type=MESH
        )
    pl.semaphore_wait(barrier, bits + int(cores))


def sum_kernel(waves, in_ref, out_ref, buf, land, full, send, recv):
    bits = bit_count(waves)
    ring = Halving(waves, buf, land, send, recv)
    greet(waves, False)
    buf[...] = in_ref[...]
    copies = []
    flying = {}
    for lane, step in diagonal(SUM_LANES, 2 * bits):
        if step:
            flying[lane].wait_recv()
        if step < bits:
            if step:
                ring.add(lane, step - 1)
            copy = ring.down(lane, step)
        else:
            if step == bits:
                spot = ring.base(lane, bits)
                full[lane, spot] = buf[lane, spot] + land[lane, 1]
            copy = ring.up(full, lane, 2 * bits - 1 - step)
        copy.start()
        flying[lane] = copy
        copies.append(copy)
    for lane in range(SUM_LANES):
        flying[lane].wait_recv()
    for copy in copies:
        copy.wait_send()
    out_ref[...] = full[...]


def backward_kernel(
    waves, off_ref, det_ref, total_ref, meas_ref, map_ref, patch_ref, probe_ref, left_ref, right_ref,
    term_ref, place_ref, grad_s, row_s, far_s, half_s, pad_s,
):
    side = probe_ref.shape[1]
    obj_side = pad_s.shape[2]
    margin = obj_side - side
    bits = bit_count(waves)
    height = side // waves
    for piece in range(2 * waves):
        chunk, half = piece // 2, piece % 2
        rows = pl.ds(piece * (height // 2), height // 2)
        total = jnp.concatenate(
            [total_ref[lane, slot_of(chunk, lane, bits)] for lane in range(half, SUM_LANES, 2)],
            axis=1,
        )
        factor = 1.0 - meas_ref[rows, :].astype(F32) / jnp.sqrt(total * (1.0 / waves) + 1.0)
        for c in range(2):
            there = pl.ds(c * side + piece * (height // 2), height // 2)
            grad_s[there, :] = (factor * det_ref[there, :]).astype(BF16)
    for c in range(2):
        pad_s[c, pl.ds(0, margin), :] = jnp.zeros((margin, obj_side), F32)
        pad_s[c, pl.ds(margin + side, margin + 16), :] = jnp.zeros((margin + 16, obj_side), F32)
    step = 256
    per = side // step
    for t in range(2 * per):
        out = dot(grad_s[pl.ds(t * step, step), :], map_ref[...])
        row_s[pl.ds((t % per) * step, step), pl.ds((t // per) * side, side)] = out.astype(BF16)
    for t in range(per):
        rows = pl.ds(t * step, step)
        far_s[rows, :] = dot(map_ref[:, t * step : (t + 1) * step], row_s[...], ((0,), (0,))).astype(BF16)
    for t in range(per):
        rows = pl.ds(t * step, step)
        out = dot(far_s[rows, :], left_ref[...]).astype(BF16)
        half_s[rows, :] = out[:, :side]
        half_s[pl.ds(side + t * step, step), :] = out[:, side:]
    shift = off_ref[1, 0]
    scale = 1.0 / waves
    fill = jnp.zeros((step, margin), F32)
    for t in range(per):
        rows = pl.ds(t * step, step)
        er = dot(right_ref[rows, :], half_s[...])
        ei = dot(right_ref[pl.ds(side + t * step, step), :], half_s[...])
        ar, ai = patch_ref[0, rows, :], patch_ref[1, rows, :]
        term_ref[0, rows, :] = ar * er + ai * ei
        term_ref[1, rows, :] = ar * ei - ai * er
        pr, pi = probe_ref[0, rows, :], probe_ref[1, rows, :]
        real = (pr * er + pi * ei) * scale
        imag = (pr * ei - pi * er) * scale
        pad_s[0, pl.ds(margin + t * step, step), :] = pltpu.roll(
            jnp.concatenate([real, fill], axis=1), shift, axis=1
        )
        pad_s[1, pl.ds(margin + t * step, step), :] = pltpu.roll(
            jnp.concatenate([imag, fill], axis=1), shift, axis=1
        )
    tall = place_ref.shape[3]
    wide = place_ref.shape[4]
    first = margin - off_ref[0, 0]
    for c in range(2):
        for owner in range(2 * waves):
            start = first + owner * tall
            tiles = (tall + 7) // 8 * 8 + 8
            block = pad_s[c, pl.ds(pl.multiple_of(start // 8 * 8, 8), tiles), :]
            block = pltpu.roll(block, lax.rem(tiles - start % 8, tiles), axis=0)[:tall]
            for part in range(place_ref.shape[1] // 2):
                lane = 2 * part + c
                place_ref[owner % 2, lane, slot_of(owner // 2, lane, bits)] = block[
                    :, part * wide : (part + 1) * wide
                ]


def scatter_kernel(
    waves, place_ref, obj_ref, buf, land, cross, send, recv, csend, crecv
):
    bits = bit_count(waves)
    ring = Halving(waves, buf, land, send, recv)
    mine = lax.axis_index("pos")
    greet(waves, True)

    def to_core(source, target, index):
        return pltpu.make_async_remote_copy(
            src_ref=source, dst_ref=target, send_sem=csend.at[index], recv_sem=crecv.at[index],
            device_id={"pos": 1 - mine}, device_id_type=MESH,
        )

    lanes = place_ref.shape[1]
    swaps = [to_core(place_ref.at[1 - mine, lane], cross.at[lane], lane) for lane in range(lanes)]
    copies = list(swaps)
    for copy in copies:
        copy.start()
    flying = {}
    for lane, step in diagonal(lanes, bits):
        if step:
            flying[lane].wait_recv()
            ring.add(lane, step - 1)
        else:
            swaps[lane].wait_recv()
            for k in range(waves):
                buf[lane, k] = place_ref[mine, lane, k] + cross[lane, k]
        copy = ring.down(lane, step)
        copy.start()
        flying[lane] = copy
        copies.append(copy)
    wide = buf.shape[3]
    for lane in range(lanes):
        flying[lane].wait_recv()
        spot = ring.base(lane, bits)
        obj_ref[lane % 2, :, pl.ds((lane // 2) * wide, wide)] = buf[lane, spot] + land[lane, 1]
    for copy in copies:
        copy.wait_send()


def local(waves, object_field, probe_field, resample_blocks, band_start, measured, offsets):
    side = probe_field.shape[2]
    obj_side = object_field.shape[1]
    bits = bit_count(waves)
    left, right = dft_tables(side)
    probe = probe_field[0]
    vmem = pl.BlockSpec(memory_space=pltpu.VMEM)
    smem = pl.BlockSpec(memory_space=pltpu.SMEM)
    shape = jax.ShapeDtypeStruct
    plain = pltpu.CompilerParams(vmem_limit_bytes=VMEM_BYTES)
    lanes_shape = (SUM_LANES, waves, side // waves // 2, side // (SUM_LANES // 2))
    patch, det, dense, inten = pl.pallas_call(
        functools.partial(forward_kernel, waves),
        out_shape=(
            shape((2, side, side), F32), shape((2 * side, side), F32), shape((side, side), BF16),
            shape(lanes_shape, F32),
        ),
        in_specs=[smem, smem] + [vmem] * 5,
        out_specs=(vmem,) * 4,
        scratch_shapes=[
            pltpu.VMEM((2 * side, side), BF16), pltpu.VMEM((side, 2 * side), BF16),
            pltpu.VMEM((side, 2 * side), BF16), pltpu.VMEM((2 * side, side), BF16),
        ],
        compiler_params=plain,
        name="forward",
    )(offsets, band_start, object_field, probe, resample_blocks[0], left, right)
    total = pl.pallas_call(
        functools.partial(sum_kernel, waves),
        out_shape=shape(lanes_shape, F32),
        in_specs=[vmem],
        out_specs=vmem,
        scratch_shapes=[
            pltpu.VMEM(lanes_shape, F32), pltpu.VMEM(lanes_shape, F32), pltpu.VMEM(lanes_shape, F32),
            pltpu.SemaphoreType.DMA((SUM_LANES, 2 * bits)),
            pltpu.SemaphoreType.DMA((SUM_LANES, 2 * bits)),
        ],
        compiler_params=pltpu.CompilerParams(
            vmem_limit_bytes=VMEM_BYTES, collective_id=0, has_side_effects=True
        ),
        name="intensity_sum",
    )(inten)
    tall = obj_side // (2 * waves)
    wide = 128
    lanes = 2 * obj_side // wide
    place_shape = (lanes, waves, tall, wide)
    term, place = pl.pallas_call(
        functools.partial(backward_kernel, waves),
        out_shape=(shape((2, side, side), F32), shape((2,) + place_shape, F32)),
        in_specs=[smem] + [vmem] * 8,
        out_specs=(vmem,) * 2,
        scratch_shapes=[
            pltpu.VMEM((2 * side, side), BF16), pltpu.VMEM((side, 2 * side), BF16),
            pltpu.VMEM((side, 2 * side), BF16), pltpu.VMEM((2 * side, side), BF16),
            pltpu.VMEM((2, 2 * obj_side - side + 16, obj_side), F32),
        ],
        compiler_params=plain,
        name="backward",
    )(offsets, det, total, measured[0], dense, patch, probe, left, right)
    probe_grad = lax.psum(term, "pos")
    object_grad = pl.pallas_call(
        functools.partial(scatter_kernel, waves),
        out_shape=shape((2, tall, obj_side), F32),
        in_specs=[vmem],
        out_specs=vmem,
        scratch_shapes=[
            pltpu.VMEM(place_shape, F32), pltpu.VMEM(place_shape, F32), pltpu.VMEM(place_shape, F32),
            pltpu.SemaphoreType.DMA((lanes, bits)), pltpu.SemaphoreType.DMA((lanes, bits)),
            pltpu.SemaphoreType.DMA((lanes,)), pltpu.SemaphoreType.DMA((lanes,)),
        ],
        compiler_params=pltpu.CompilerParams(
            vmem_limit_bytes=VMEM_BYTES, collective_id=1, has_side_effects=True
        ),
        name="object_sum",
    )(place)
    return object_grad, probe_grad[None]


def solution(mesh):
    in_specs = (
        P(None, "parts", None),
        P("wave", None, "parts", None),
        P("wave", None, None, None),
        P("wave", None),
        P("pos", "parts", None),
        P("parts", "pos"),
    )
    out_specs = (P(None, ("parts", "wave", "pos"), None), P("wave", None, "parts", None))
    step = functools.partial(local, mesh.shape["wave"])
    return jax.shard_map(step, mesh=mesh, in_specs=in_specs, out_specs=out_specs, check_vma=False)
```
